128 devices in a mesh: tile: 16 (over x, y), scan: 8 (over z, core).
Axes of the slice: x: 4, y: 4, z: 4, core: 2. Of those that a mesh axis runs over, the one named last changes fastest.
Arguments:
- object_field: float32 [2, 16384, 1024], P(None, 'tile'), may hold values from -6 to 6
- probe: float32 [2, 512, 512], replicated, may hold values from -6 to 6
- amplitudes: float32 [384, 512, 512], P(('tile', 'scan')), may hold values from 0 to 3
- corners: int32 [384, 2], P(('tile', 'scan')), may hold values from 0 to 16383, as said below
Outputs:
- object_gradient: float32 [2, 16384, 1024], P(None, 'tile')
- probe_gradient: float32 [2, 512, 512], replicated
The draws below stay inside these ranges and needn't reach their ends.
Inputs may be any that keep to these rules, and one draw needn't show every extreme that they name: `corners`: pattern n belongs to tile n // 24, and its corner row lies in that tile's rows: from (n // 24) * 1024 to that plus 1024 - 1; its corner column lies in 0 to 512.
All inputs are finite; a program needn't handle non-finite values.
Results may differ from the reference program's by a relative error of at most 0.0003.
Values sent between devices are 32-bit elements; how exact they have to be, the bound alone decides.
No kernel may reach another device: no remote copies, remote signals or barrier semaphores. Data moves between devices by JAX's collectives and lax.ppermute only.
A program may use at most 192 MiB of HBM per device.

```python
import jax
import jax.numpy as jnp
from jax import lax

P_SIZE = 512
ROWS_DEV = 1024
OBJ_COLS = 1024
PER_TILE = 24
PATTERNS = 384
OBJ_ROWS = 16384


def draw_corners(key, part):
    key = jax.random.fold_in(key, 7)
    row_key, col_key = jax.random.split(key)
    pattern_index = jnp.arange(PATTERNS, dtype=jnp.int32)
    owner_tile = pattern_index // PER_TILE
    within = pattern_index % PER_TILE
    row_offset = jax.random.randint(row_key, (PATTERNS,), 0, ROWS_DEV, dtype=jnp.int32)
    row_offset = jnp.where(within == 0, ROWS_DEV - 1, jnp.where(within == 1, 0, row_offset))
    col_starts = jax.random.randint(col_key, (PATTERNS,), 0, OBJ_COLS - P_SIZE + 1, dtype=jnp.int32)
    col_starts = jnp.where(within == 0, 0, jnp.where(within == 1, OBJ_COLS - P_SIZE, col_starts))
    row_starts = owner_tile * ROWS_DEV + row_offset
    return jnp.stack([row_starts, col_starts], axis=1).astype(jnp.int32)


def steps_of(own_key, shape, shards, smallest, top_value):
    level, own = 1.0, jax.random.fold_in(own_key, 6)
    for axis_at, parts in shards:
        draws = jnp.exp(jax.random.uniform(jax.random.fold_in(own, axis_at), (parts,), jnp.float32, smallest / len(shards), top_value / len(shards)))
        level = level * jnp.repeat(draws, shape[axis_at] // parts).reshape([-1 if axis == axis_at else 1 for axis in range(len(shape))])
    return level


def bell_draw(rng, shape, scale, bound, cuts=(), kind=jnp.bfloat16):
    entries = jax.random.normal(rng, shape, jnp.float32) * scale
    if len(cuts) > 0:
        entries = steps_of(rng, shape, cuts, -0.22, 0.18) * entries
    return jnp.clip(entries, min=-bound, max=bound).astype(kind)


def setup_inputs(seed: int = 0) -> dict:
    arg_keys = jax.random.split(jax.random.key(seed), 5)
    object_field = bell_draw(arg_keys[0], (2, OBJ_ROWS, OBJ_COLS), 1.0, 6.0, ((1, 16),), jnp.float32)
    probe = bell_draw(arg_keys[1], (2, P_SIZE, P_SIZE), 1.0, 6.0, (), jnp.float32)
    amplitudes = jnp.clip(3.0 * jax.random.uniform(arg_keys[2], (PATTERNS, P_SIZE, P_SIZE), jnp.float32) ** steps_of(arg_keys[2], (PATTERNS, P_SIZE, P_SIZE), ((0, 128),), -0.2, 0.2), 0.0, 3.0)
    corners = draw_corners(jax.random.fold_in(arg_keys[4], 71), 0)
    return dict(object_field=object_field, probe=probe, amplitudes=amplitudes, corners=corners)


def reference(object_field, probe, amplitudes, corners):
    padded = jnp.concatenate([object_field, jnp.zeros((2, P_SIZE, OBJ_COLS), object_field.dtype)], axis=1)
    probe_complex = probe[0] + 1j * probe[1]

    def accumulate(totals, pattern_item):
        object_grad, probe_grad = totals
        amplitude, corner = pattern_item
        anchor = (jnp.zeros((), jnp.int32), corner[0].astype(jnp.int32), corner[1].astype(jnp.int32))
        patch = lax.dynamic_slice(padded, anchor, (2, P_SIZE, P_SIZE))
        patch_complex = patch[0] + 1j * patch[1]
        far_field = jnp.fft.fft2(probe_complex * patch_complex, norm='ortho')
        modulus = jnp.sqrt(far_field.real * far_field.real + far_field.imag * far_field.imag + 1.0)
        exit_error = jnp.fft.ifft2(far_field * (1.0 - amplitude / modulus), norm='ortho')
        object_term = jnp.conj(probe_complex) * exit_error
        probe_term = jnp.conj(patch_complex) * exit_error
        previous = lax.dynamic_slice(object_grad, anchor, (2, P_SIZE, P_SIZE))
        object_grad = lax.dynamic_update_slice(object_grad, previous + jnp.stack([object_term.real, object_term.imag]).astype(object_grad.dtype), anchor)
        probe_grad = probe_grad + jnp.stack([probe_term.real, probe_term.imag]).astype(probe_grad.dtype)
        return ((object_grad, probe_grad), None)
    start_totals = (jnp.zeros(padded.shape, jnp.float32), jnp.zeros((2, P_SIZE, P_SIZE), jnp.float32))
    (object_grad, probe_grad), unused = lax.scan(accumulate, start_totals, (amplitudes, corners))
    return (object_grad[:, :OBJ_ROWS, :], probe_grad)
```

```python
import functools
import math

import jax
import jax.numpy as jnp
import ml_dtypes
import numpy as np
from jax import lax
from jax.experimental import pallas as pl
from jax.experimental.pallas import tpu as pltpu
from jax.sharding import Mesh, PartitionSpec as P

SIDE = 512
QUART = 128
COLS = 1024
STRIP = 1024
SPAN = STRIP + SIDE
SLICE = 64
CHUNK = 64
PAT = 3
ROUTE = (
    (2, 0, 0, (0, 0)),
    (1, 1, 0, (0, 1)),
    (3, 0, 0, (1, 0)),
    (2, 1, 0, (1, 1)),
    (1, 0, 1, (0,)),
    (3, 1, 1, (1,)),
    (0, 0, 1, (2,)),
    (0, 1, 1, (3,)),
)
BF = jnp.bfloat16
F32 = jnp.float32


def quarter_tables():
    k0 = np.arange(4)[:, None, None]
    k1 = np.arange(QUART)[None, :, None]
    i0 = np.arange(QUART)[None, None, :]
    phase = ((4 * k1 + k0) * i0) % SIDE
    angle = phase.astype(np.float64) * (2.0 * math.pi / SIDE)
    real = np.cos(angle) / math.sqrt(SIDE)
    imag = -np.sin(angle) / math.sqrt(SIDE)
    form = np.concatenate(
        [np.concatenate([real, -imag], axis=2), np.concatenate([imag, real], axis=2)], axis=1
    ).astype(np.float32)

    def parts(table):
        high = table.astype(ml_dtypes.bfloat16)
        low = (table - high.astype(np.float32)).astype(ml_dtypes.bfloat16)
        return np.stack([high, low])

    return parts(form), parts(np.ascontiguousarray(np.swapaxes(form, 1, 2)))


def order_matrix():
    index = np.arange(SIDE)
    order = 4 * (index % QUART) + index // QUART
    return (order[:, None] == index[None, :]).astype(np.float32)


def split(value):
    high = value.astype(BF)
    return high, (value - high.astype(F32)).astype(BF)


def dot3(left_high, left_low, right_high, right_low):
    dot = functools.partial(jnp.dot, preferred_element_type=F32)
    return dot(left_high, right_high) + (dot(left_high, right_low) + dot(left_low, right_high))


def radix4(parts, sign):
    (r0, i0), (r1, i1), (r2, i2), (r3, i3) = parts
    ar, ai, br, bi = r0 + r2, i0 + i2, r0 - r2, i0 - i2
    cr, ci, dr, di = r1 + r3, i1 + i3, r1 - r3, i1 - i3
    plus = (br - di, bi + dr)
    minus = (br + di, bi - dr)
    first, third = (plus, minus) if sign > 0 else (minus, plus)
    return [(ar + cr, ai + ci), first, (ar - cr, ai - ci), third]


def patterns_kernel(where, strip, *refs):
    halo = refs[:10]
    probe, amps, form, flip = refs[10:14]
    sends = refs[14:22]
    probe_sum = refs[22]
    ext, win, patch, high, low, real, sems = refs[23:]
    z = where[6]
    core = where[7]

    copies = []

    def start(src, dst):
        copy = pltpu.make_async_copy(src, dst, sems.at[len(copies)])
        copy.start()
        copies.append(copy)

    start(strip, ext.at[:, pl.ds(0, STRIP), :])
    for half, owner in ((0, core), (1, 1 - core)):
        pieces = halo[5 * half : 5 * half + 5]

        def place(q):
            row = STRIP + lax.rem(z + q, 4) * (2 * SLICE) + owner * SLICE
            return pl.ds(pl.multiple_of(row, SLICE), SLICE)

        start(pieces[0], ext.at[:, place(0), :])
        start(pieces[1], ext.at[:, place(3), :])
        start(pieces[2], ext.at[:, place(1), :])
        start(pieces[3], ext.at[0, place(2), :])
        start(pieces[4], ext.at[1, place(2), :])

    def clear(step, carry):
        win[:, pl.ds(pl.multiple_of(step * CHUNK, CHUNK), CHUNK), :] = jnp.zeros((2, CHUNK, COLS), F32)
        return carry

    lax.fori_loop(0, SPAN // CHUNK, clear, 0)
    probe_sum[...] = jnp.zeros_like(probe_sum)
    for copy in copies:
        copy.wait()

    def one_pattern(p, carry):
        row = where[2 * p]
        col = where[2 * p + 1]
        row8 = pl.multiple_of((row // 8) * 8, 8)
        col128 = pl.multiple_of(jnp.minimum((col // QUART) * QUART, COLS - SIDE - QUART), QUART)
        row_off = row - row8
        col_off = col - col128

        def cut(step, carry):
            base = pl.multiple_of(step * CHUNK, CHUNK)
            rows = pl.ds(base, CHUNK)
            cuts = []
            for plane in range(2):
                block = ext[plane, pl.ds(pl.multiple_of(row8 + base, 8), CHUNK + 8), pl.ds(col128, SIDE + QUART)]
                block = pltpu.roll(block, lax.rem(CHUNK + 8 - row_off, CHUNK + 8), 0)[:CHUNK]
                block = pltpu.roll(block, lax.rem(SIDE + QUART - col_off, SIDE + QUART), 1)[:, :SIDE]
                patch[plane, rows, :] = block
                cuts.append(block)
            pr, pi = probe[0, rows, :], probe[1, rows, :]
            wr = pr * cuts[0] - pi * cuts[1]
            wi = pr * cuts[1] + pi * cuts[0]
            terms = radix4([(wr[:, n * QUART : (n + 1) * QUART], wi[:, n * QUART : (n + 1) * QUART]) for n in range(4)], -1)
            for n, (tr, ti) in enumerate(terms):
                hr, lr = split(tr)
                hi, li = split(ti)
                high[n, rows, :QUART] = hr
                high[n, rows, QUART:] = hi
                low[n, rows, :QUART] = lr
                low[n, rows, QUART:] = li
            return carry

        lax.fori_loop(0, SIDE // CHUNK, cut, 0)

        for n in range(4):
            real[pl.ds(n * SIDE, SIDE), :] = dot3(high[n], low[n], flip[0, n], flip[1, n])

        for n in range(4):
            lanes = pl.ds((n % 2) * QUART, QUART)

            def rows_in(step, carry):
                base = pl.multiple_of(step * 32, 32)
                parts = []
                for m in range(4):
                    block = real[pl.ds(pl.multiple_of(n * SIDE + m * QUART + base, 32), 32), :]
                    parts.append((block[:, :QUART], block[:, QUART:]))
                for m, (tr, ti) in enumerate(radix4(parts, -1)):
                    hr, lr = split(tr)
                    hi, li = split(ti)
                    at_re = pl.ds(pl.multiple_of((n // 2) * 256 + base, 32), 32)
                    at_im = pl.ds(pl.multiple_of((n // 2) * 256 + QUART + base, 32), 32)
                    high[m, at_re, lanes] = hr
                    high[m, at_im, lanes] = hi
                    low[m, at_re, lanes] = lr
                    low[m, at_im, lanes] = li
                return carry

            lax.fori_loop(0, QUART // 32, rows_in, 0)

        for m in range(4):
            for half in range(2):
                at = pl.ds(half * 256, 256)
                far = dot3(form[0, m], form[1, m], high[m, at, :], low[m, at, :])
                fr, fi = far[:QUART], far[QUART:]
                amp = amps[p, pl.ds(m * QUART, QUART), pl.ds(half * 256, 256)]
                factor = 1.0 - amp * lax.rsqrt(fr * fr + fi * fi + 1.0)
                hr, lr = split(fr * factor)
                hi, li = split(fi * factor)
                right_high = jnp.concatenate([hr, hi], axis=0)
                right_low = jnp.concatenate([lr, li], axis=0)
                real[pl.ds(m * SIDE + half * 256, 256), :] = dot3(flip[0, m], flip[1, m], right_high, right_low)

        for n in range(4):
            half, lane = n // 2, (n % 2) * QUART

            def rows_out(step, carry):
                base = pl.multiple_of(step * 32, 32)
                parts = []
                for m in range(4):
                    at_re = pl.ds(pl.multiple_of(m * SIDE + half * 256 + base, 32), 32)
                    at_im = pl.ds(pl.multiple_of(m * SIDE + half * 256 + QUART + base, 32), 32)
                    parts.append((real[at_re, pl.ds(lane, QUART)], real[at_im, pl.ds(lane, QUART)]))
                for m, (tr, ti) in enumerate(radix4(parts, 1)):
                    hr, lr = split(tr)
                    hi, li = split(ti)
                    at = pl.ds(pl.multiple_of(m * QUART + base, 32), 32)
                    high[n, at, :QUART] = hr
                    high[n, at, QUART:] = hi
                    low[n, at, :QUART] = lr
                    low[n, at, QUART:] = li
                return carry

            lax.fori_loop(0, QUART // 32, rows_out, 0)

        for n in range(4):
            real[pl.ds(n * SIDE, SIDE), :] = dot3(high[n], low[n], form[0, n], form[1, n])

        def finish(step, carry):
            base = pl.multiple_of(step * CHUNK, CHUNK)
            rows = pl.ds(base, CHUNK)
            parts = []
            for n in range(4):
                block = real[pl.ds(pl.multiple_of(n * SIDE + base, CHUNK), CHUNK), :]
                parts.append((block[:, :QUART], block[:, QUART:]))
            blocks = radix4(parts, 1)
            er = jnp.concatenate([b[0] for b in blocks], axis=1)
            ei = jnp.concatenate([b[1] for b in blocks], axis=1)
            qr, qi = patch[0, rows, :], patch[1, rows, :]
            probe_sum[0, rows, :] += qr * er + qi * ei
            probe_sum[1, rows, :] += qr * ei - qi * er
            pr, pi = probe[0, rows, :], probe[1, rows, :]
            terms = (pr * er + pi * ei, pr * ei - pi * er)
            for plane in range(2):
                wide = jnp.concatenate([terms[plane], jnp.zeros((CHUNK, QUART), F32)], axis=1)
                wide = pltpu.roll(wide, col_off, 1)
                tall = jnp.concatenate([wide, jnp.zeros((8, SIDE + QUART), F32)], axis=0)
                tall = pltpu.roll(tall, row_off, 0)
                at = (plane, pl.ds(pl.multiple_of(row8 + base, 8), CHUNK + 8), pl.ds(col128, SIDE + QUART))
                win[at] = win[at] + tall
            return carry

        lax.fori_loop(0, SIDE // CHUNK, finish, 0)
        return carry

    lax.fori_loop(0, PAT, one_pattern, 0)

    first = len(copies)
    for zone in (2, 0, 1):
        for j, plane, group, at in ROUTE:
            top = zone * SIDE + lax.rem(z + j, 4) * (2 * SLICE)
            for which, owner in ((0, 1 - core), (1, core)):
                rows = pl.ds(pl.multiple_of(top + owner * SLICE, SLICE), SLICE)
                dst = sends[6 + which].at[at + (zone,)] if group else sends[2 * zone + which].at[at]
                start(win.at[plane, rows, :], dst)
    for copy in copies[first:]:
        copy.wait()


def run_patterns(where, strip, halo, probe, amps):
    form, flip = quarter_tables()
    hbm = pl.BlockSpec(memory_space=pl.ANY)
    vmem = pl.BlockSpec(memory_space=pltpu.VMEM)
    smem = pl.BlockSpec(memory_space=pltpu.SMEM)
    leads = [(2, 2)] * 6 + [(4, 3)] * 2
    part = [jax.ShapeDtypeStruct(lead + (SLICE, COLS), F32) for lead in leads]
    return pl.pallas_call(
        patterns_kernel,
        out_shape=part + [jax.ShapeDtypeStruct((2, SIDE, SIDE), F32)],
        in_specs=[smem, hbm] + [hbm] * 10 + [vmem] * 4,
        out_specs=[hbm] * 8 + [vmem],
        scratch_shapes=[
            pltpu.VMEM((2, SPAN, COLS), F32),
            pltpu.VMEM((2, SPAN, COLS), F32),
            pltpu.VMEM((2, SIDE, SIDE), F32),
            pltpu.VMEM((4, SIDE, 256), BF),
            pltpu.VMEM((4, SIDE, 256), BF),
            pltpu.VMEM((4 * SIDE, 256), F32),
            pltpu.SemaphoreType.DMA((64,)),
        ],
        compiler_params=pltpu.CompilerParams(vmem_limit_bytes=56 * 1024 * 1024),
        cost_estimate=pl.CostEstimate(flops=2 * 4_831_838_208, bytes_accessed=40_000_000, transcendentals=786_432),
    )(where, strip, *halo, probe, amps, jnp.asarray(form), jnp.asarray(flip))


def ring(axis, step):
    size = lax.axis_size(axis)
    return [(i, (i + step) % size) for i in range(size)]


def z_up(block):
    return lax.ppermute(block, "z", ring("z", 1))


def z_down(block):
    return lax.ppermute(block, "z", ring("z", -1))


def swap(block):
    return lax.ppermute(block, "core", [(0, 1), (1, 0)])


def along_tiles(block, step):
    tiles = lax.axis_size("x") * lax.axis_size("y")
    return lax.ppermute(block, ("x", "y"), [(i, i + step) for i in range(tiles) if 0 <= i + step < tiles])


def spread(own):
    below = z_up(own)
    above = z_down(own)
    return [own, below, above, z_up(below[0]), z_down(above[1])]


def first_half(theirs, mine):
    both = mine + swap(theirs)
    return z_up(both[0]), z_down(both[1])


def second_half(both, from_below, from_above):
    last_below = z_up(both[0] + from_below[0])
    last_above = z_down(both[1] + from_above[1])
    return both[2] + from_above[0] + last_below, both[3] + from_below[1] + last_above


def others(block, axis):
    return [lax.ppermute(block, axis, ring(axis, -step)) for step in (1, 2, 3)]


def in_order(block, axis, rest=None):
    here = lax.axis_index(axis)
    four = jnp.stack([block] + (rest or others(block, axis)), axis=1)
    four = lax.dynamic_slice_in_dim(jnp.concatenate([four, four], axis=1), lax.rem(4 - here, 4), 4, 1)
    return four.reshape(2, -1, block.shape[2])


def share_of_sum(part, axis):
    here = lax.axis_index(axis)
    cut = part.reshape(2, 4, -1, part.shape[2])
    mine = lax.dynamic_index_in_dim(cut, here, 1, keepdims=False)
    return mine, [
        lax.ppermute(
            lax.dynamic_index_in_dim(cut, lax.rem(here + step, 4), 1, keepdims=False), axis, ring(axis, step)
        )
        for step in (1, 2, 3)
    ]


def on_device(object_field, probe, amplitudes, corners):
    z = lax.axis_index("z")
    core = lax.axis_index("core")
    tile = lax.axis_index("x") * lax.axis_size("y") + lax.axis_index("y")
    local = corners - jnp.array([1, 0], jnp.int32) * (tile * STRIP)
    where = jnp.concatenate([local.reshape(-1), jnp.stack([z, core]).astype(jnp.int32)])

    share = lax.dynamic_slice(
        object_field, (0, z * (2 * SLICE) + core * SLICE, 0), (2, SLICE, COLS)
    )
    order = jnp.asarray(order_matrix())
    product = functools.partial(jnp.einsum, precision=lax.Precision.HIGH)
    amps = product("nkl,ml->nkm", product("mk,nkl->nml", order, amplitudes), order)
    shifted, amps = lax.optimization_barrier((along_tiles(share, -1), amps))
    pieces = spread(shifted)
    halo = pieces + [swap(piece) for piece in pieces]

    *sends, theirs2, mine2, probe_sum = run_patterns(where, object_field, halo, probe, amps)

    tie = lax.optimization_barrier
    halves = probe_sum.reshape(2, 2, SIDE // 2, SIDE)
    part = lax.dynamic_index_in_dim(halves, core, 1, keepdims=False)
    part = part + swap(lax.dynamic_index_in_dim(halves, 1 - core, 1, keepdims=False))

    first_low = first_half(sends[4], sends[5])
    first_top = first_half(sends[0], sends[1])
    first_mid = first_half(sends[2], sends[3])
    both2 = mine2 + swap(theirs2)
    first_low, part = tie((first_low, part))
    low = second_half(both2[:, 2], *first_low)
    part, pieces = share_of_sum(part, "y")
    first_top, part, pieces = tie((first_top, part, pieces))
    part, pieces = share_of_sum(sum(pieces, part), "x")
    first_mid, part, pieces, low = tie((first_mid, part, pieces, low))
    carried = along_tiles(jnp.stack(low), 1)
    below, above = (jnp.stack(pair, axis=1) for pair in zip(first_top, first_mid))
    part = sum(pieces, part)
    below, above, part, pieces = tie((below, above, part, others(part, "z")))
    part = in_order(sum(pieces, part), "x")
    re, im = second_half(both2[:, :2], below, above)
    re, im, part, carried = tie((re, im, part, carried))

    re = re.at[0].add(carried[0])
    im = im.at[0].add(carried[1])
    re, im = tie((re, im))
    below_re, above_im = z_up(re), z_down(im)
    below_im, above_re = z_up(im), z_down(re)
    opposite_re, opposite_im = z_up(below_re), z_down(above_im)
    found = (
        (re, 0, 0), (im, 1, 0),
        (below_re, 0, 3), (above_im, 1, 1), (below_im, 1, 3), (above_re, 0, 1),
        (opposite_re, 0, 2), (opposite_im, 1, 2),
    )
    opposite_re, opposite_im, part, pieces = tie((opposite_re, opposite_im, part, others(part, "y")))
    part = in_order(part, "y", pieces)
    other = swap(part)
    probe_gradient = jnp.concatenate([
        jnp.where(core == 0, part, other), jnp.where(core == 0, other, part)
    ], axis=1)
    whole = jnp.zeros((2, 2, 4, 2, SLICE, COLS), F32)

    def put(whole, block, plane, shift, owner):
        at = (plane, 0, lax.rem(z + shift, 4), owner, 0, 0)
        return lax.dynamic_update_slice(whole, block[None, :, None, None], at)

    for group in (found[:6], found[6:]):
        for block, plane, shift in group:
            whole = put(whole, block, plane, shift, core)
        for block, plane, shift in group:
            whole = put(whole, swap(block), plane, shift, 1 - core)
    return (whole.reshape(2, STRIP, COLS), probe_gradient)


def solution(mesh):
    tiles, scans = mesh.devices.shape
    side = math.isqrt(tiles)
    fine = Mesh(mesh.devices.reshape(side, tiles // side, scans // 2, 2), ("x", "y", "z", "core"))
    placed = (
        P(None, ("x", "y"), None),
        P(),
        P(("x", "y", "z", "core"), None, None),
        P(("x", "y", "z", "core"), None),
    )
    return jax.shard_map(
        on_device,
        mesh=fine,
        in_specs=placed,
        out_specs=(P(None, ("x", "y"), None), P()),
        check_vma=False,
    )
```

```python
import functools
import math

import jax
import jax.numpy as jnp
import ml_dtypes
import numpy as np
from jax import lax
from jax.experimental import pallas as pl
from jax.experimental.pallas import tpu as pltpu
from jax.sharding import Mesh, PartitionSpec as P

SIDE = 512
QUART = 128
COLS = 1024
STRIP = 1024
SPAN = STRIP + SIDE
SLICE = 64
CHUNK = 64
PAT = 3
HALO = ((0, 0), (1, 0), (0, 3), (1, 3), (0, 1), (1, 1), (0, 2), (1, 2))
ROUTE = (
    (2, 0, 0, (0, 0)),
    (1, 1, 0, (0, 1)),
    (3, 0, 0, (1, 0)),
    (2, 1, 0, (1, 1)),
    (1, 0, 1, (0,)),
    (3, 1, 1, (1,)),
    (0, 0, 1, (2,)),
    (0, 1, 1, (3,)),
)
BF = jnp.bfloat16
F32 = jnp.float32


def quarter_tables():
    k0 = np.arange(4)[:, None, None]
    k1 = np.arange(QUART)[None, :, None]
    i0 = np.arange(QUART)[None, None, :]
    phase = ((4 * k1 + k0) * i0) % SIDE
    angle = phase.astype(np.float64) * (2.0 * math.pi / SIDE)
    real = np.cos(angle) / math.sqrt(SIDE)
    imag = -np.sin(angle) / math.sqrt(SIDE)
    form = np.concatenate(
        [np.concatenate([real, -imag], axis=2), np.concatenate([imag, real], axis=2)], axis=1
    ).astype(np.float32)

    def parts(table):
        high = table.astype(ml_dtypes.bfloat16)
        low = (table - high.astype(np.float32)).astype(ml_dtypes.bfloat16)
        return np.stack([high, low])

    return parts(form), parts(np.ascontiguousarray(np.swapaxes(form, 1, 2)))


def order_matrix():
    index = np.arange(SIDE)
    order = 4 * (index % QUART) + index // QUART
    return (order[:, None] == index[None, :]).astype(np.float32)


def split(value):
    high = value.astype(BF)
    return high, (value - high.astype(F32)).astype(BF)


def dot3(left_high, left_low, right_high, right_low):
    dot = functools.partial(jnp.dot, preferred_element_type=F32)
    return dot(left_high, right_high) + (dot(left_high, right_low) + dot(left_low, right_high))


def radix4(parts, sign):
    (r0, i0), (r1, i1), (r2, i2), (r3, i3) = parts
    ar, ai, br, bi = r0 + r2, i0 + i2, r0 - r2, i0 - i2
    cr, ci, dr, di = r1 + r3, i1 + i3, r1 - r3, i1 - i3
    plus = (br - di, bi + dr)
    minus = (br + di, bi - dr)
    first, third = (plus, minus) if sign > 0 else (minus, plus)
    return [(ar + cr, ai + ci), first, (ar - cr, ai - ci), third]


def patterns_kernel(where, strip, *refs):
    halo = refs[:16]
    probe_hbm, amps_hbm, form_hbm, flip_hbm = refs[16:20]
    sends = refs[20:28]
    probe_sum = refs[28]
    ext, win, patch, high, low, high2, low2, real, real2, probe, amps, form, flip, sems = refs[29:]
    z = where[6]
    core = where[7]

    copies = []

    def start(src, dst):
        copy = pltpu.make_async_copy(src, dst, sems.at[len(copies)])
        copy.start()
        copies.append(copy)

    start(probe_hbm, probe)
    start(strip, ext.at[:, pl.ds(0, STRIP), :])
    for half, owner in ((0, core), (1, 1 - core)):
        for n, (plane, shift) in enumerate(HALO):
            row = STRIP + lax.rem(z + shift, 4) * (2 * SLICE) + owner * SLICE
            start(halo[8 * half + n], ext.at[plane, pl.ds(pl.multiple_of(row, SLICE), SLICE), :])

    early = len(copies)
    for src, dst in ((flip_hbm, flip), (form_hbm, form), (amps_hbm, amps)):
        start(src, dst)

    def clear(step, carry):
        win[:, pl.ds(pl.multiple_of(step * CHUNK, CHUNK), CHUNK), :] = jnp.zeros((2, CHUNK, COLS), F32)
        return carry

    lax.fori_loop(0, SPAN // CHUNK, clear, 0)
    probe_sum[...] = jnp.zeros_like(probe_sum)
    for copy in copies[:early]:
        copy.wait()

    def one_pattern(p, carry):
        row = where[2 * p]
        col = where[2 * p + 1]
        row8 = pl.multiple_of((row // 8) * 8, 8)
        col128 = pl.multiple_of(jnp.minimum((col // QUART) * QUART, COLS - SIDE - QUART), QUART)
        row_off = row - row8
        col_off = col - col128

        def cut(step, carry):
            base = pl.multiple_of(step * CHUNK, CHUNK)
            rows = pl.ds(base, CHUNK)
            cuts = []
            for plane in range(2):
                block = ext[plane, pl.ds(pl.multiple_of(row8 + base, 8), CHUNK + 8), pl.ds(col128, SIDE + QUART)]
                block = pltpu.roll(block, lax.rem(CHUNK + 8 - row_off, CHUNK + 8), 0)[:CHUNK]
                block = pltpu.roll(block, lax.rem(SIDE + QUART - col_off, SIDE + QUART), 1)[:, :SIDE]
                patch[plane, rows, :] = block
                cuts.append(block)
            pr, pi = probe[0, rows, :], probe[1, rows, :]
            wr = pr * cuts[0] - pi * cuts[1]
            wi = pr * cuts[1] + pi * cuts[0]
            terms = radix4([(wr[:, n * QUART : (n + 1) * QUART], wi[:, n * QUART : (n + 1) * QUART]) for n in range(4)], -1)
            for n, (tr, ti) in enumerate(terms):
                hr, lr = split(tr)
                hi, li = split(ti)
                high[n, rows, :QUART] = hr
                high[n, rows, QUART:] = hi
                low[n, rows, :QUART] = lr
                low[n, rows, QUART:] = li
            return carry

        lax.fori_loop(0, SIDE // CHUNK, cut, 0, unroll=True)

        @pl.when(p == 0)
        def _():
            for copy in copies[early : early + 3]:
                copy.wait()


        for n in range(4):
            real[pl.ds(n * SIDE, SIDE), :] = dot3(high[n], low[n], flip[0, n], flip[1, n])
            lanes = pl.ds((n % 2) * QUART, QUART)

            def rows_in(step, carry):
                base = pl.multiple_of(step * 32, 32)
                parts = []
                for m in range(4):
                    block = real[pl.ds(pl.multiple_of(n * SIDE + m * QUART + base, 32), 32), :]
                    parts.append((block[:, :QUART], block[:, QUART:]))
                for m, (tr, ti) in enumerate(radix4(parts, -1)):
                    hr, lr = split(tr)
                    hi, li = split(ti)
                    at_re = pl.ds(pl.multiple_of((n // 2) * 256 + base, 32), 32)
                    at_im = pl.ds(pl.multiple_of((n // 2) * 256 + QUART + base, 32), 32)
                    high2[m, at_re, lanes] = hr
                    high2[m, at_im, lanes] = hi
                    low2[m, at_re, lanes] = lr
                    low2[m, at_im, lanes] = li
                return carry

            lax.fori_loop(0, QUART // 32, rows_in, 0, unroll=True)

        for m in range(4):
            for half in range(2):
                at = pl.ds(half * 256, 256)
                far = dot3(form[0, m], form[1, m], high2[m, at, :], low2[m, at, :])
                fr, fi = far[:QUART], far[QUART:]
                amp = amps[p, pl.ds(m * QUART, QUART), pl.ds(half * 256, 256)]
                factor = 1.0 - amp * lax.rsqrt(fr * fr + fi * fi + 1.0)
                hr, lr = split(fr * factor)
                hi, li = split(fi * factor)
                right_high = jnp.concatenate([hr, hi], axis=0)
                right_low = jnp.concatenate([lr, li], axis=0)
                real2[pl.ds(m * SIDE + half * 256, 256), :] = dot3(flip[0, m], flip[1, m], right_high, right_low)

        for n in range(4):
            half, lane = n // 2, (n % 2) * QUART

            def rows_out(step, carry):
                base = pl.multiple_of(step * 32, 32)
                parts = []
                for m in range(4):
                    at_re = pl.ds(pl.multiple_of(m * SIDE + half * 256 + base, 32), 32)
                    at_im = pl.ds(pl.multiple_of(m * SIDE + half * 256 + QUART + base, 32), 32)
                    parts.append((real2[at_re, pl.ds(lane, QUART)], real2[at_im, pl.ds(lane, QUART)]))
                for m, (tr, ti) in enumerate(radix4(parts, 1)):
                    hr, lr = split(tr)
                    hi, li = split(ti)
                    at = pl.ds(pl.multiple_of(m * QUART + base, 32), 32)
                    high[n, at, :QUART] = hr
                    high[n, at, QUART:] = hi
                    low[n, at, :QUART] = lr
                    low[n, at, QUART:] = li
                return carry

            lax.fori_loop(0, QUART // 32, rows_out, 0, unroll=True)
            real[pl.ds(n * SIDE, SIDE), :] = dot3(high[n], low[n], form[0, n], form[1, n])

        def finish(step, carry):
            base = pl.multiple_of(step * CHUNK, CHUNK)
            rows = pl.ds(base, CHUNK)
            parts = []
            for n in range(4):
                block = real[pl.ds(pl.multiple_of(n * SIDE + base, CHUNK), CHUNK), :]
                parts.append((block[:, :QUART], block[:, QUART:]))
            blocks = radix4(parts, 1)
            er = jnp.concatenate([b[0] for b in blocks], axis=1)
            ei = jnp.concatenate([b[1] for b in blocks], axis=1)
            qr, qi = patch[0, rows, :], patch[1, rows, :]
            probe_sum[0, rows, :] += qr * er + qi * ei
            probe_sum[1, rows, :] += qr * ei - qi * er
            pr, pi = probe[0, rows, :], probe[1, rows, :]
            terms = (pr * er + pi * ei, pr * ei - pi * er)
            for plane in range(2):
                wide = jnp.concatenate([terms[plane], jnp.zeros((CHUNK, QUART), F32)], axis=1)
                wide = pltpu.roll(wide, col_off, 1)
                tall = jnp.concatenate([wide, jnp.zeros((8, SIDE + QUART), F32)], axis=0)
                tall = pltpu.roll(tall, row_off, 0)
                at = (plane, pl.ds(pl.multiple_of(row8 + base, 8), CHUNK + 8), pl.ds(col128, SIDE + QUART))
                win[at] = win[at] + tall
            return carry

        lax.fori_loop(0, SIDE // CHUNK, finish, 0, unroll=True)
        return carry

    lax.fori_loop(0, PAT, one_pattern, 0)

    first = len(copies)
    for zone in (2, 0, 1):
        for j, plane, group, at in ROUTE:
            top = zone * SIDE + lax.rem(z + j, 4) * (2 * SLICE)
            for which, owner in ((0, 1 - core), (1, core)):
                rows = pl.ds(pl.multiple_of(top + owner * SLICE, SLICE), SLICE)
                dst = sends[6 + which].at[at + (zone,)] if group else sends[2 * zone + which].at[at]
                start(win.at[plane, rows, :], dst)
    for copy in copies[first:]:
        copy.wait()


def run_patterns(where, strip, halo, probe, amps):
    form, flip = quarter_tables()
    hbm = pl.BlockSpec(memory_space=pl.ANY)
    vmem = pl.BlockSpec(memory_space=pltpu.VMEM)
    smem = pl.BlockSpec(memory_space=pltpu.SMEM)
    leads = [(2, 2)] * 6 + [(4, 3)] * 2
    part = [jax.ShapeDtypeStruct(lead + (SLICE, COLS), F32) for lead in leads]
    return pl.pallas_call(
        patterns_kernel,
        out_shape=part + [jax.ShapeDtypeStruct((2, SIDE, SIDE), F32)],
        in_specs=[smem] + [hbm] * 21,
        out_specs=[hbm] * 8 + [vmem],
        scratch_shapes=[
            pltpu.VMEM((2, SPAN, COLS), F32),
            pltpu.VMEM((2, SPAN, COLS), F32),
            pltpu.VMEM((2, SIDE, SIDE), F32),
            pltpu.VMEM((4, SIDE, 256), BF),
            pltpu.VMEM((4, SIDE, 256), BF),
            pltpu.VMEM((4, SIDE, 256), BF),
            pltpu.VMEM((4, SIDE, 256), BF),
            pltpu.VMEM((4 * SIDE, 256), F32),
            pltpu.VMEM((4 * SIDE, 256), F32),
            pltpu.VMEM((2, SIDE, SIDE), F32),
            pltpu.VMEM((PAT, SIDE, SIDE), F32),
            pltpu.VMEM((2, 4, 256, 256), BF),
            pltpu.VMEM((2, 4, 256, 256), BF),
            pltpu.SemaphoreType.DMA((80,)),
        ],
        compiler_params=pltpu.CompilerParams(vmem_limit_bytes=56 * 1024 * 1024),
        cost_estimate=pl.CostEstimate(flops=2 * 4_831_838_208, bytes_accessed=40_000_000, transcendentals=786_432),
    )(where, strip, *halo, probe, amps, jnp.asarray(form), jnp.asarray(flip))


def ring(axis, step):
    size = lax.axis_size(axis)
    return [(i, (i + step) % size) for i in range(size)]


def z_up(block):
    return lax.ppermute(block, "z", ring("z", 1))


def z_down(block):
    return lax.ppermute(block, "z", ring("z", -1))


def swap(block):
    return lax.ppermute(block, "core", [(0, 1), (1, 0)])


def along_tiles(block, step):
    tiles = lax.axis_size("x") * lax.axis_size("y")
    return lax.ppermute(block, ("x", "y"), [(i, i + step) for i in range(tiles) if 0 <= i + step < tiles])


def first_half(theirs, mine):
    both = mine + swap(theirs)
    return z_up(both[0]), z_down(both[1])


def second_half(both, from_below, from_above):
    last_below = z_up(both[0] + from_below[0])
    last_above = z_down(both[1] + from_above[1])
    return both[2] + from_above[0] + last_below, both[3] + from_below[1] + last_above


def others(block, axis):
    return [lax.ppermute(block, axis, ring(axis, -step)) for step in (1, 2, 3)]


def in_order(block, axis, rest=None):
    here = lax.axis_index(axis)
    four = jnp.stack([block] + (rest or others(block, axis)), axis=1)
    four = lax.dynamic_slice_in_dim(jnp.concatenate([four, four], axis=1), lax.rem(4 - here, 4), 4, 1)
    return four.reshape(2, -1, block.shape[2])


def share_of_sum(part, axis):
    here = lax.axis_index(axis)
    cut = part.reshape(2, 4, -1, part.shape[2])
    mine = lax.dynamic_index_in_dim(cut, here, 1, keepdims=False)
    return mine, [
        lax.ppermute(
            lax.dynamic_index_in_dim(cut, lax.rem(here + step, 4), 1, keepdims=False), axis, ring(axis, step)
        )
        for step in (1, 2, 3)
    ]


def on_device(object_field, probe, amplitudes, corners):
    z = lax.axis_index("z")
    core = lax.axis_index("core")
    tile = lax.axis_index("x") * lax.axis_size("y") + lax.axis_index("y")
    local = corners - jnp.array([1, 0], jnp.int32) * (tile * STRIP)
    where = jnp.concatenate([local.reshape(-1), jnp.stack([z, core]).astype(jnp.int32)])

    share = lax.dynamic_slice(
        object_field, (0, z * (2 * SLICE) + core * SLICE, 0), (2, SLICE, COLS)
    )
    order = jnp.asarray(order_matrix())
    product = functools.partial(jnp.einsum, precision=lax.Precision.HIGH)
    amps = product("nkl,ml->nkm", product("mk,nkl->nml", order, amplitudes), order)
    tie = lax.optimization_barrier
    re = along_tiles(share[0], -1)
    im = along_tiles(share[1], -1)
    below_re, above_re = z_up(re), z_down(re)
    below_im, above_im = z_up(im), z_down(im)
    below_re, above_re, amps = tie((below_re, above_re, amps))
    halo = [re, im, below_re, below_im, above_re, above_im, z_up(below_re), z_down(above_im)]
    halo += [swap(piece) for piece in halo]

    *sends, theirs2, mine2, probe_sum = run_patterns(where, object_field, halo, probe, amps)

    halves = probe_sum.reshape(2, 2, SIDE // 2, SIDE)
    part = lax.dynamic_index_in_dim(halves, core, 1, keepdims=False)
    part = part + swap(lax.dynamic_index_in_dim(halves, 1 - core, 1, keepdims=False))

    first_low = first_half(sends[4], sends[5])
    first_top = first_half(sends[0], sends[1])
    first_mid = first_half(sends[2], sends[3])
    both2 = mine2 + swap(theirs2)
    first_low, part = tie((first_low, part))
    low = second_half(both2[:, 2], *first_low)
    part, pieces = share_of_sum(part, "y")
    first_top, part, pieces = tie((first_top, part, pieces))
    part, pieces = share_of_sum(sum(pieces, part), "x")
    first_mid, part, pieces, low = tie((first_mid, part, pieces, low))
    carried = along_tiles(jnp.stack(low), 1)
    below, above = (jnp.stack(pair, axis=1) for pair in zip(first_top, first_mid))
    part = sum(pieces, part)
    below, above, part, pieces = tie((below, above, part, others(part, "z")))
    part = in_order(sum(pieces, part), "x")
    re, im = second_half(both2[:, :2], below, above)
    re, im, part, carried = tie((re, im, part, carried))

    re = re.at[0].add(carried[0])
    im = im.at[0].add(carried[1])
    re, im = tie((re, im))
    below_re, above_im = z_up(re), z_down(im)
    below_im, above_re = z_up(im), z_down(re)
    opposite_re, opposite_im = z_up(below_re), z_down(above_im)
    found = (
        (re, 0, 0), (im, 1, 0),
        (below_re, 0, 3), (above_im, 1, 1), (below_im, 1, 3), (above_re, 0, 1),
        (opposite_re, 0, 2), (opposite_im, 1, 2),
    )
    opposite_re, opposite_im, part, pieces = tie((opposite_re, opposite_im, part, others(part, "y")))
    part = in_order(part, "y", pieces)
    other = swap(part)
    probe_gradient = jnp.concatenate([
        jnp.where(core == 0, part, other), jnp.where(core == 0, other, part)
    ], axis=1)
    whole = jnp.zeros((2, 2, 4, 2, SLICE, COLS), F32)

    def put(whole, block, plane, shift, owner):
        at = (plane, 0, lax.rem(z + shift, 4), owner, 0, 0)
        return lax.dynamic_update_slice(whole, block[None, :, None, None], at)

    for group in (found[:6], found[6:]):
        for block, plane, shift in group:
            whole = put(whole, block, plane, shift, core)
        for block, plane, shift in group:
            whole = put(whole, swap(block), plane, shift, 1 - core)
    return (whole.reshape(2, STRIP, COLS), probe_gradient)


def solution(mesh):
    tiles, scans = mesh.devices.shape
    side = math.isqrt(tiles)
    fine = Mesh(mesh.devices.reshape(side, tiles // side, scans // 2, 2), ("x", "y", "z", "core"))
    placed = (
        P(None, ("x", "y"), None),
        P(),
        P(("x", "y", "z", "core"), None, None),
        P(("x", "y", "z", "core"), None),
    )
    return jax.shard_map(
        on_device,
        mesh=fine,
        in_specs=placed,
        out_specs=(P(None, ("x", "y"), None), P()),
        check_vma=False,
    )
```

```python
import functools
import math

import jax
import jax.numpy as jnp
import ml_dtypes
import numpy as np
from jax import lax
from jax.experimental import pallas as pl
from jax.experimental.pallas import tpu as pltpu
from jax.sharding import Mesh, PartitionSpec as P

SIDE = 512
QUART = 128
COLS = 1024
STRIP = 1024
SPAN = STRIP + SIDE
SLICE = 64
CHUNK = 64
PAT = 3
HALO = ((0, 0), (1, 0), (0, 3), (1, 3), (0, 1), (1, 1), (0, 2), (1, 2))
ROUTE = (
    (2, 0, 0, (0, 0)),
    (1, 1, 0, (0, 1)),
    (3, 0, 0, (1, 0)),
    (2, 1, 0, (1, 1)),
    (1, 0, 1, (0,)),
    (3, 1, 1, (1,)),
    (0, 0, 1, (2,)),
    (0, 1, 1, (3,)),
)
BF = jnp.bfloat16
F32 = jnp.float32


def quarter_tables():
    k0 = np.arange(4)[:, None, None]
    k1 = np.arange(QUART)[None, :, None]
    i0 = np.arange(QUART)[None, None, :]
    phase = ((4 * k1 + k0) * i0) % SIDE
    angle = phase.astype(np.float64) * (2.0 * math.pi / SIDE)
    real = np.cos(angle) / math.sqrt(SIDE)
    imag = -np.sin(angle) / math.sqrt(SIDE)
    form = np.concatenate(
        [np.concatenate([real, -imag], axis=2), np.concatenate([imag, real], axis=2)], axis=1
    ).astype(np.float32)

    def parts(table):
        high = table.astype(ml_dtypes.bfloat16)
        low = (table - high.astype(np.float32)).astype(ml_dtypes.bfloat16)
        return np.stack([high, low])

    return parts(form), parts(np.ascontiguousarray(np.swapaxes(form, 1, 2)))


def order_matrix():
    index = np.arange(SIDE)
    order = 4 * (index % QUART) + index // QUART
    return (order[:, None] == index[None, :]).astype(np.float32)


def split(value):
    high = value.astype(BF)
    return high, (value - high.astype(F32)).astype(BF)


def dot3(left_high, left_low, right_high, right_low):
    dot = functools.partial(jnp.dot, preferred_element_type=F32)
    return dot(left_high, right_high) + (dot(left_high, right_low) + dot(left_low, right_high))


def radix4(parts, sign):
    (r0, i0), (r1, i1), (r2, i2), (r3, i3) = parts
    ar, ai, br, bi = r0 + r2, i0 + i2, r0 - r2, i0 - i2
    cr, ci, dr, di = r1 + r3, i1 + i3, r1 - r3, i1 - i3
    plus = (br - di, bi + dr)
    minus = (br + di, bi - dr)
    first, third = (plus, minus) if sign > 0 else (minus, plus)
    return [(ar + cr, ai + ci), first, (ar - cr, ai - ci), third]


def patterns_kernel(where, strip, *refs):
    halo = refs[:16]
    probe_hbm, amps_hbm, form_hbm, flip_hbm = refs[16:20]
    sends = refs[20:28]
    probe_sum = refs[28]
    ext, win, patch, high, low, high2, low2, real, real2, probe, amps, form, flip, sems = refs[29:]
    z = where[6]
    core = where[7]

    copies = []

    def start(src, dst):
        copy = pltpu.make_async_copy(src, dst, sems.at[len(copies)])
        copy.start()
        copies.append(copy)

    start(probe_hbm, probe)
    start(strip, ext.at[:, pl.ds(0, STRIP), :])
    for half, owner in ((0, core), (1, 1 - core)):
        for n, (plane, shift) in enumerate(HALO):
            row = STRIP + lax.rem(z + shift, 4) * (2 * SLICE) + owner * SLICE
            start(halo[8 * half + n], ext.at[plane, pl.ds(pl.multiple_of(row, SLICE), SLICE), :])

    early = len(copies)
    for src, dst in ((flip_hbm, flip), (form_hbm, form), (amps_hbm, amps)):
        start(src, dst)

    def clear(step, carry):
        win[:, pl.ds(pl.multiple_of(step * CHUNK, CHUNK), CHUNK), :] = jnp.zeros((2, CHUNK, COLS), F32)
        return carry

    lax.fori_loop(0, SPAN // CHUNK, clear, 0)
    probe_sum[...] = jnp.zeros_like(probe_sum)
    for copy in copies[:early]:
        copy.wait()

    outs = []
    for zone in (2, 0, 1):
        for j, plane, group, at in ROUTE:
            top = zone * SIDE + lax.rem(z + j, 4) * (2 * SLICE)
            for which, owner in ((0, 1 - core), (1, core)):
                base = top + owner * SLICE
                rows = pl.ds(pl.multiple_of(base, SLICE), SLICE)
                dst = sends[6 + which].at[at + (zone,)] if group else sends[2 * zone + which].at[at]
                copy = pltpu.make_async_copy(win.at[plane, rows, :], dst, sems.at[len(copies) + len(outs)])
                outs.append((copy, base))
    last_row = (where[2 * PAT - 2] // 8) * 8

    def touched(base):
        return (base + SLICE > last_row) & (base < last_row + SIDE + 8)

    def one_pattern(p, carry):
        @pl.when(p == PAT - 1)
        def _():
            for copy, base in outs:
                pl.when(jnp.logical_not(touched(base)))(copy.start)

        row = where[2 * p]
        col = where[2 * p + 1]
        row8 = pl.multiple_of((row // 8) * 8, 8)
        col128 = pl.multiple_of(jnp.minimum((col // QUART) * QUART, COLS - SIDE - QUART), QUART)
        row_off = row - row8
        col_off = col - col128

        def cut(step, carry):
            base = pl.multiple_of(step * CHUNK, CHUNK)
            rows = pl.ds(base, CHUNK)
            cuts = []
            for plane in range(2):
                block = ext[plane, pl.ds(pl.multiple_of(row8 + base, 8), CHUNK + 8), pl.ds(col128, SIDE + QUART)]
                block = pltpu.roll(block, lax.rem(CHUNK + 8 - row_off, CHUNK + 8), 0)[:CHUNK]
                block = pltpu.roll(block, lax.rem(SIDE + QUART - col_off, SIDE + QUART), 1)[:, :SIDE]
                patch[plane, rows, :] = block
                cuts.append(block)
            pr, pi = probe[0, rows, :], probe[1, rows, :]
            wr = pr * cuts[0] - pi * cuts[1]
            wi = pr * cuts[1] + pi * cuts[0]
            terms = radix4([(wr[:, n * QUART : (n + 1) * QUART], wi[:, n * QUART : (n + 1) * QUART]) for n in range(4)], -1)
            for n, (tr, ti) in enumerate(terms):
                hr, lr = split(tr)
                hi, li = split(ti)
                high[n, rows, :QUART] = hr
                high[n, rows, QUART:] = hi
                low[n, rows, :QUART] = lr
                low[n, rows, QUART:] = li
            return carry

        lax.fori_loop(0, SIDE // CHUNK, cut, 0, unroll=True)

        @pl.when(p == 0)
        def _():
            for copy in copies[early : early + 3]:
                copy.wait()


        for n in range(4):
            real[pl.ds(n * SIDE, SIDE), :] = dot3(high[n], low[n], flip[0, n], flip[1, n])
            lanes = pl.ds((n % 2) * QUART, QUART)

            def rows_in(step, carry):
                base = pl.multiple_of(step * 32, 32)
                parts = []
                for m in range(4):
                    block = real[pl.ds(pl.multiple_of(n * SIDE + m * QUART + base, 32), 32), :]
                    parts.append((block[:, :QUART], block[:, QUART:]))
                for m, (tr, ti) in enumerate(radix4(parts, -1)):
                    hr, lr = split(tr)
                    hi, li = split(ti)
                    at_re = pl.ds(pl.multiple_of((n // 2) * 256 + base, 32), 32)
                    at_im = pl.ds(pl.multiple_of((n // 2) * 256 + QUART + base, 32), 32)
                    high2[m, at_re, lanes] = hr
                    high2[m, at_im, lanes] = hi
                    low2[m, at_re, lanes] = lr
                    low2[m, at_im, lanes] = li
                return carry

            lax.fori_loop(0, QUART // 32, rows_in, 0, unroll=True)

        for m in range(4):
            for half in range(2):
                at = pl.ds(half * 256, 256)
                far = dot3(form[0, m], form[1, m], high2[m, at, :], low2[m, at, :])
                fr, fi = far[:QUART], far[QUART:]
                amp = amps[p, pl.ds(m * QUART, QUART), pl.ds(half * 256, 256)]
                factor = 1.0 - amp * lax.rsqrt(fr * fr + fi * fi + 1.0)
                hr, lr = split(fr * factor)
                hi, li = split(fi * factor)
                right_high = jnp.concatenate([hr, hi], axis=0)
                right_low = jnp.concatenate([lr, li], axis=0)
                real2[pl.ds(m * SIDE + half * 256, 256), :] = dot3(flip[0, m], flip[1, m], right_high, right_low)

        for n in range(4):
            half, lane = n // 2, (n % 2) * QUART

            def rows_out(step, carry):
                base = pl.multiple_of(step * 32, 32)
                parts = []
                for m in range(4):
                    at_re = pl.ds(pl.multiple_of(m * SIDE + half * 256 + base, 32), 32)
                    at_im = pl.ds(pl.multiple_of(m * SIDE + half * 256 + QUART + base, 32), 32)
                    parts.append((real2[at_re, pl.ds(lane, QUART)], real2[at_im, pl.ds(lane, QUART)]))
                for m, (tr, ti) in enumerate(radix4(parts, 1)):
                    hr, lr = split(tr)
                    hi, li = split(ti)
                    at = pl.ds(pl.multiple_of(m * QUART + base, 32), 32)
                    high[n, at, :QUART] = hr
                    high[n, at, QUART:] = hi
                    low[n, at, :QUART] = lr
                    low[n, at, QUART:] = li
                return carry

            lax.fori_loop(0, QUART // 32, rows_out, 0, unroll=True)
            real[pl.ds(n * SIDE, SIDE), :] = dot3(high[n], low[n], form[0, n], form[1, n])

        def finish(step, carry):
            base = pl.multiple_of(step * CHUNK, CHUNK)
            rows = pl.ds(base, CHUNK)
            parts = []
            for n in range(4):
                block = real[pl.ds(pl.multiple_of(n * SIDE + base, CHUNK), CHUNK), :]
                parts.append((block[:, :QUART], block[:, QUART:]))
            blocks = radix4(parts, 1)
            er = jnp.concatenate([b[0] for b in blocks], axis=1)
            ei = jnp.concatenate([b[1] for b in blocks], axis=1)
            qr, qi = patch[0, rows, :], patch[1, rows, :]
            probe_sum[0, rows, :] += qr * er + qi * ei
            probe_sum[1, rows, :] += qr * ei - qi * er
            pr, pi = probe[0, rows, :], probe[1, rows, :]
            terms = (pr * er + pi * ei, pr * ei - pi * er)
            for plane in range(2):
                wide = jnp.concatenate([terms[plane], jnp.zeros((CHUNK, QUART), F32)], axis=1)
                wide = pltpu.roll(wide, col_off, 1)
                tall = jnp.concatenate([wide, jnp.zeros((8, SIDE + QUART), F32)], axis=0)
                tall = pltpu.roll(tall, row_off, 0)
                at = (plane, pl.ds(pl.multiple_of(row8 + base, 8), CHUNK + 8), pl.ds(col128, SIDE + QUART))
                win[at] = win[at] + tall
            return carry

        lax.fori_loop(0, SIDE // CHUNK, finish, 0, unroll=True)
        return carry

    lax.fori_loop(0, PAT, one_pattern, 0)

    for copy, base in outs:
        pl.when(touched(base))(copy.start)
    for copy, base in outs:
        copy.wait()


def run_patterns(where, strip, halo, probe, amps):
    form, flip = quarter_tables()
    hbm = pl.BlockSpec(memory_space=pl.ANY)
    vmem = pl.BlockSpec(memory_space=pltpu.VMEM)
    smem = pl.BlockSpec(memory_space=pltpu.SMEM)
    leads = [(2, 2)] * 6 + [(4, 3)] * 2
    part = [jax.ShapeDtypeStruct(lead + (SLICE, COLS), F32) for lead in leads]
    return pl.pallas_call(
        patterns_kernel,
        out_shape=part + [jax.ShapeDtypeStruct((2, SIDE, SIDE), F32)],
        in_specs=[smem] + [hbm] * 21,
        out_specs=[hbm] * 8 + [vmem],
        scratch_shapes=[
            pltpu.VMEM((2, SPAN, COLS), F32),
            pltpu.VMEM((2, SPAN, COLS), F32),
            pltpu.VMEM((2, SIDE, SIDE), F32),
            pltpu.VMEM((4, SIDE, 256), BF),
            pltpu.VMEM((4, SIDE, 256), BF),
            pltpu.VMEM((4, SIDE, 256), BF),
            pltpu.VMEM((4, SIDE, 256), BF),
            pltpu.VMEM((4 * SIDE, 256), F32),
            pltpu.VMEM((4 * SIDE, 256), F32),
            pltpu.VMEM((2, SIDE, SIDE), F32),
            pltpu.VMEM((PAT, SIDE, SIDE), F32),
            pltpu.VMEM((2, 4, 256, 256), BF),
            pltpu.VMEM((2, 4, 256, 256), BF),
            pltpu.SemaphoreType.DMA((80,)),
        ],
        compiler_params=pltpu.CompilerParams(vmem_limit_bytes=56 * 1024 * 1024),
        cost_estimate=pl.CostEstimate(flops=2 * 4_831_838_208, bytes_accessed=40_000_000, transcendentals=786_432),
    )(where, strip, *halo, probe, amps, jnp.asarray(form), jnp.asarray(flip))


def ring(axis, step):
    size = lax.axis_size(axis)
    return [(i, (i + step) % size) for i in range(size)]


def z_up(block):
    return lax.ppermute(block, "z", ring("z", 1))


def z_down(block):
    return lax.ppermute(block, "z", ring("z", -1))


def swap(block):
    return lax.ppermute(block, "core", [(0, 1), (1, 0)])


def along_tiles(block, step):
    tiles = lax.axis_size("x") * lax.axis_size("y")
    return lax.ppermute(block, ("x", "y"), [(i, i + step) for i in range(tiles) if 0 <= i + step < tiles])


def first_half(theirs, mine):
    both = mine + swap(theirs)
    return z_up(both[0]), z_down(both[1])


def second_half(both, from_below, from_above):
    last = (z_up(both[0] + from_below[0]), z_down(both[1] + from_above[1]))
    last_below, last_above = lax.optimization_barrier(last)
    return both[2] + from_above[0] + last_below, both[3] + from_below[1] + last_above


def others(block, axis):
    return [lax.ppermute(block, axis, ring(axis, -step)) for step in (1, 2, 3)]


def in_order(block, axis, rest=None):
    here = lax.axis_index(axis)
    four = jnp.stack([block] + (rest or others(block, axis)), axis=1)
    four = lax.dynamic_slice_in_dim(jnp.concatenate([four, four], axis=1), lax.rem(4 - here, 4), 4, 1)
    return four.reshape(2, -1, block.shape[2])


def share_of_sum(part, axis):
    here = lax.axis_index(axis)
    cut = part.reshape(2, 4, -1, part.shape[2])
    mine = lax.dynamic_index_in_dim(cut, here, 1, keepdims=False)
    return mine, [
        lax.ppermute(
            lax.dynamic_index_in_dim(cut, lax.rem(here + step, 4), 1, keepdims=False), axis, ring(axis, step)
        )
        for step in (1, 2, 3)
    ]


def on_device(object_field, probe, amplitudes, corners):
    z = lax.axis_index("z")
    core = lax.axis_index("core")
    tile = lax.axis_index("x") * lax.axis_size("y") + lax.axis_index("y")
    local = corners - jnp.array([1, 0], jnp.int32) * (tile * STRIP)
    where = jnp.concatenate([local.reshape(-1), jnp.stack([z, core]).astype(jnp.int32)])

    share = lax.dynamic_slice(
        object_field, (0, z * (2 * SLICE) + core * SLICE, 0), (2, SLICE, COLS)
    )
    order = jnp.asarray(order_matrix())
    product = functools.partial(jnp.einsum, precision=lax.Precision.HIGH)
    amps = product("nkl,ml->nkm", product("mk,nkl->nml", order, amplitudes), order)
    tie = lax.optimization_barrier
    re = along_tiles(share[0], -1)
    im = along_tiles(share[1], -1)
    below_re, above_re = z_up(re), z_down(re)
    below_im, above_im = z_up(im), z_down(im)
    below_re, above_re, amps = tie((below_re, above_re, amps))
    halo = [re, im, below_re, below_im, above_re, above_im, z_up(below_re), z_down(above_im)]
    halo += [swap(piece) for piece in halo]

    *sends, theirs2, mine2, probe_sum = run_patterns(where, object_field, halo, probe, amps)

    halves = probe_sum.reshape(2, 2, SIDE // 2, SIDE)
    part = lax.dynamic_index_in_dim(halves, core, 1, keepdims=False)
    part = part + swap(lax.dynamic_index_in_dim(halves, 1 - core, 1, keepdims=False))

    first_low = first_half(sends[4], sends[5])
    first_top = first_half(sends[0], sends[1])
    first_mid = first_half(sends[2], sends[3])
    both2 = mine2 + swap(theirs2)
    first_low, part = tie((first_low, part))
    low = second_half(both2[:, 2], *first_low)
    part, pieces = share_of_sum(part, "y")
    first_top, part, pieces = tie((first_top, part, pieces))
    part, pieces = share_of_sum(sum(pieces, part), "x")
    first_mid, part, pieces, low = tie((first_mid, part, pieces, low))
    carried = along_tiles(jnp.stack(low), 1)
    below, above = (jnp.stack(pair, axis=1) for pair in zip(first_top, first_mid))
    part = sum(pieces, part)
    below, above, part, pieces = tie((below, above, part, others(part, "z")))
    part = in_order(sum(pieces, part), "x")
    re, im = second_half(both2[:, :2], below, above)
    re, im, part, carried = tie((re, im, part, carried))

    re = re.at[0].add(carried[0])
    im = im.at[0].add(carried[1])
    re, im = tie((re, im))
    below_re, above_im = z_up(re), z_down(im)
    below_im, above_re = z_up(im), z_down(re)
    opposite_re, opposite_im = z_up(below_re), z_down(above_im)
    found = (
        (re, 0, 0), (im, 1, 0),
        (below_re, 0, 3), (above_im, 1, 1), (below_im, 1, 3), (above_re, 0, 1),
        (opposite_re, 0, 2), (opposite_im, 1, 2),
    )
    opposite_re, opposite_im, part, pieces = tie((opposite_re, opposite_im, part, others(part, "y")))
    part = in_order(part, "y", pieces)
    other = swap(part)
    probe_gradient = jnp.concatenate([
        jnp.where(core == 0, part, other), jnp.where(core == 0, other, part)
    ], axis=1)
    whole = jnp.zeros((2, 2, 4, 2, SLICE, COLS), F32)

    def put(whole, block, plane, shift, owner):
        at = (plane, 0, lax.rem(z + shift, 4), owner, 0, 0)
        return lax.dynamic_update_slice(whole, block[None, :, None, None], at)

    for group in (found[:6], found[6:]):
        for block, plane, shift in group:
            whole = put(whole, block, plane, shift, core)
        for block, plane, shift in group:
            whole = put(whole, swap(block), plane, shift, 1 - core)
    return (whole.reshape(2, STRIP, COLS), probe_gradient)


def solution(mesh):
    tiles, scans = mesh.devices.shape
    side = math.isqrt(tiles)
    fine = Mesh(mesh.devices.reshape(side, tiles // side, scans // 2, 2), ("x", "y", "z", "core"))
    placed = (
        P(None, ("x", "y"), None),
        P(),
        P(("x", "y", "z", "core"), None, None),
        P(("x", "y", "z", "core"), None),
    )
    return jax.shard_map(
        on_device,
        mesh=fine,
        in_specs=placed,
        out_specs=(P(None, ("x", "y"), None), P()),
        check_vma=False,
    )
```

```python
import functools
import math

import jax
import jax.numpy as jnp
import ml_dtypes
import numpy as np
from jax import lax
from jax.experimental import pallas as pl
from jax.experimental.pallas import tpu as pltpu
from jax.sharding import Mesh, PartitionSpec as P

SIDE = 512
QUART = 128
COLS = 1024
STRIP = 1024
SPAN = STRIP + SIDE
SLICE = 64
CHUNK = 64
PAT = 3
HALO = ((0, 0), (1, 0), (0, 3), (1, 3), (0, 1), (1, 1), (0, 2), (1, 2))
ROUTE = (
    (2, 0, 0, (0, 0)),
    (1, 1, 0, (0, 1)),
    (3, 0, 0, (1, 0)),
    (2, 1, 0, (1, 1)),
    (1, 0, 1, (0,)),
    (3, 1, 1, (1,)),
    (0, 0, 1, (2,)),
    (0, 1, 1, (3,)),
)
BF = jnp.bfloat16
F32 = jnp.float32


def quarter_tables():
    k0 = np.arange(4)[:, None, None]
    k1 = np.arange(QUART)[None, :, None]
    i0 = np.arange(QUART)[None, None, :]
    phase = ((4 * k1 + k0) * i0) % SIDE
    angle = phase.astype(np.float64) * (2.0 * math.pi / SIDE)
    real = np.cos(angle) / math.sqrt(SIDE)
    imag = -np.sin(angle) / math.sqrt(SIDE)
    form = np.concatenate(
        [np.concatenate([real, -imag], axis=2), np.concatenate([imag, real], axis=2)], axis=1
    ).astype(np.float32)

    def parts(table):
        high = table.astype(ml_dtypes.bfloat16)
        low = (table - high.astype(np.float32)).astype(ml_dtypes.bfloat16)
        return np.stack([high, low])

    return parts(form), parts(np.ascontiguousarray(np.swapaxes(form, 1, 2)))


def order_matrix():
    index = np.arange(SIDE)
    order = 4 * (index % QUART) + index // QUART
    return (order[:, None] == index[None, :]).astype(np.float32)


def split(value):
    high = value.astype(BF)
    return high, (value - high.astype(F32)).astype(BF)


def dot3(left_high, left_low, right_high, right_low):
    dot = functools.partial(jnp.dot, preferred_element_type=F32)
    return dot(left_high, right_high) + (dot(left_high, right_low) + dot(left_low, right_high))


def radix4(parts, sign):
    (r0, i0), (r1, i1), (r2, i2), (r3, i3) = parts
    ar, ai, br, bi = r0 + r2, i0 + i2, r0 - r2, i0 - i2
    cr, ci, dr, di = r1 + r3, i1 + i3, r1 - r3, i1 - i3
    plus = (br - di, bi + dr)
    minus = (br + di, bi - dr)
    first, third = (plus, minus) if sign > 0 else (minus, plus)
    return [(ar + cr, ai + ci), first, (ar - cr, ai - ci), third]


def patterns_kernel(where, strip, *refs):
    halo = refs[:16]
    probe_hbm, amps_hbm, form_hbm, flip_hbm = refs[16:20]
    sends = refs[20:28]
    probe_sum = refs[28]
    ext, win, patch, high, low, high2, low2, real, real2, probe, amps, form, flip, sems = refs[29:]
    z = where[6]
    core = where[7]

    copies = []

    def start(src, dst):
        copy = pltpu.make_async_copy(src, dst, sems.at[len(copies)])
        copy.start()
        copies.append(copy)

    start(probe_hbm, probe)
    start(strip, ext.at[:, pl.ds(0, STRIP), :])
    for half, owner in ((0, core), (1, 1 - core)):
        for n, (plane, shift) in enumerate(HALO):
            row = STRIP + lax.rem(z + shift, 4) * (2 * SLICE) + owner * SLICE
            start(halo[8 * half + n], ext.at[plane, pl.ds(pl.multiple_of(row, SLICE), SLICE), :])

    early = len(copies)
    for src, dst in ((flip_hbm, flip), (form_hbm, form), (amps_hbm, amps)):
        start(src, dst)

    def clear(step, carry):
        win[:, pl.ds(pl.multiple_of(step * CHUNK, CHUNK), CHUNK), :] = jnp.zeros((2, CHUNK, COLS), F32)
        return carry

    lax.fori_loop(0, SPAN // CHUNK, clear, 0)
    probe_sum[...] = jnp.zeros_like(probe_sum)
    for copy in copies[:early]:
        copy.wait()

    outs = []
    for zone in (2, 0, 1):
        for j, plane, group, at in ROUTE:
            top = zone * SIDE + lax.rem(z + j, 4) * (2 * SLICE)
            for which, owner in ((0, 1 - core), (1, core)):
                base = top + owner * SLICE
                rows = pl.ds(pl.multiple_of(base, SLICE), SLICE)
                dst = sends[6 + which].at[at + (zone,)] if group else sends[2 * zone + which].at[at]
                copy = pltpu.make_async_copy(win.at[plane, rows, :], dst, sems.at[len(copies) + len(outs)])
                outs.append((copy, base))
    last_row = (where[2 * PAT - 2] // 8) * 8

    def touched(base):
        return (base + SLICE > last_row) & (base < last_row + SIDE + 8)

    def one_pattern(p, carry):
        @pl.when(p == PAT - 1)
        def _():
            for copy, base in outs:
                pl.when(jnp.logical_not(touched(base)))(copy.start)

        row = where[2 * p]
        col = where[2 * p + 1]
        row8 = pl.multiple_of((row // 8) * 8, 8)
        col128 = pl.multiple_of(jnp.minimum((col // QUART) * QUART, COLS - SIDE - QUART), QUART)
        row_off = row - row8
        col_off = col - col128

        def cut(step, carry):
            base = pl.multiple_of(step * CHUNK, CHUNK)
            rows = pl.ds(base, CHUNK)
            cuts = []
            for plane in range(2):
                block = ext[plane, pl.ds(pl.multiple_of(row8 + base, 8), CHUNK + 8), pl.ds(col128, SIDE + QUART)]
                block = pltpu.roll(block, lax.rem(CHUNK + 8 - row_off, CHUNK + 8), 0)[:CHUNK]
                block = pltpu.roll(block, lax.rem(SIDE + QUART - col_off, SIDE + QUART), 1)[:, :SIDE]
                patch[plane, rows, :] = block
                cuts.append(block)
            pr, pi = probe[0, rows, :], probe[1, rows, :]
            wr = pr * cuts[0] - pi * cuts[1]
            wi = pr * cuts[1] + pi * cuts[0]
            terms = radix4([(wr[:, n * QUART : (n + 1) * QUART], wi[:, n * QUART : (n + 1) * QUART]) for n in range(4)], -1)
            for n, (tr, ti) in enumerate(terms):
                hr, lr = split(tr)
                hi, li = split(ti)
                high[n, rows, :QUART] = hr
                high[n, rows, QUART:] = hi
                low[n, rows, :QUART] = lr
                low[n, rows, QUART:] = li
            return carry

        lax.fori_loop(0, SIDE // CHUNK, cut, 0, unroll=True)

        @pl.when(p == 0)
        def _():
            for copy in copies[early : early + 3]:
                copy.wait()


        for n in range(4):
            real[pl.ds(n * SIDE, SIDE), :] = dot3(high[n], low[n], flip[0, n], flip[1, n])
            lanes = pl.ds((n % 2) * QUART, QUART)

            def rows_in(step, carry):
                base = pl.multiple_of(step * 32, 32)
                parts = []
                for m in range(4):
                    block = real[pl.ds(pl.multiple_of(n * SIDE + m * QUART + base, 32), 32), :]
                    parts.append((block[:, :QUART], block[:, QUART:]))
                for m, (tr, ti) in enumerate(radix4(parts, -1)):
                    hr, lr = split(tr)
                    hi, li = split(ti)
                    at_re = pl.ds(pl.multiple_of((n // 2) * 256 + base, 32), 32)
                    at_im = pl.ds(pl.multiple_of((n // 2) * 256 + QUART + base, 32), 32)
                    high2[m, at_re, lanes] = hr
                    high2[m, at_im, lanes] = hi
                    low2[m, at_re, lanes] = lr
                    low2[m, at_im, lanes] = li
                return carry

            lax.fori_loop(0, QUART // 32, rows_in, 0, unroll=True)

        for m in range(4):
            for half in range(2):
                at = pl.ds(half * 256, 256)
                far = dot3(form[0, m], form[1, m], high2[m, at, :], low2[m, at, :])
                fr, fi = far[:QUART], far[QUART:]
                amp = amps[p, pl.ds(m * QUART, QUART), pl.ds(half * 256, 256)]
                factor = 1.0 - amp * lax.rsqrt(fr * fr + fi * fi + 1.0)
                hr, lr = split(fr * factor)
                hi, li = split(fi * factor)
                right_high = jnp.concatenate([hr, hi], axis=0)
                right_low = jnp.concatenate([lr, li], axis=0)
                real2[pl.ds(m * SIDE + half * 256, 256), :] = dot3(flip[0, m], flip[1, m], right_high, right_low)

        for n in range(4):
            half, lane = n // 2, (n % 2) * QUART

            def rows_out(step, carry):
                base = pl.multiple_of(step * 32, 32)
                parts = []
                for m in range(4):
                    at_re = pl.ds(pl.multiple_of(m * SIDE + half * 256 + base, 32), 32)
                    at_im = pl.ds(pl.multiple_of(m * SIDE + half * 256 + QUART + base, 32), 32)
                    parts.append((real2[at_re, pl.ds(lane, QUART)], real2[at_im, pl.ds(lane, QUART)]))
                for m, (tr, ti) in enumerate(radix4(parts, 1)):
                    hr, lr = split(tr)
                    hi, li = split(ti)
                    at = pl.ds(pl.multiple_of(m * QUART + base, 32), 32)
                    high[n, at, :QUART] = hr
                    high[n, at, QUART:] = hi
                    low[n, at, :QUART] = lr
                    low[n, at, QUART:] = li
                return carry

            lax.fori_loop(0, QUART // 32, rows_out, 0, unroll=True)
            real[pl.ds(n * SIDE, SIDE), :] = dot3(high[n], low[n], form[0, n], form[1, n])

        def finish(step, carry):
            base = pl.multiple_of(step * CHUNK, CHUNK)
            rows = pl.ds(base, CHUNK)
            parts = []
            for n in range(4):
                block = real[pl.ds(pl.multiple_of(n * SIDE + base, CHUNK), CHUNK), :]
                parts.append((block[:, :QUART], block[:, QUART:]))
            blocks = radix4(parts, 1)
            er = jnp.concatenate([b[0] for b in blocks], axis=1)
            ei = jnp.concatenate([b[1] for b in blocks], axis=1)
            qr, qi = patch[0, rows, :], patch[1, rows, :]
            probe_sum[0, rows, :] += qr * er + qi * ei
            probe_sum[1, rows, :] += qr * ei - qi * er
            pr, pi = probe[0, rows, :], probe[1, rows, :]
            terms = (pr * er + pi * ei, pr * ei - pi * er)
            for plane in range(2):
                wide = jnp.concatenate([terms[plane], jnp.zeros((CHUNK, QUART), F32)], axis=1)
                wide = pltpu.roll(wide, col_off, 1)
                tall = jnp.concatenate([wide, jnp.zeros((8, SIDE + QUART), F32)], axis=0)
                tall = pltpu.roll(tall, row_off, 0)
                at = (plane, pl.ds(pl.multiple_of(row8 + base, 8), CHUNK + 8), pl.ds(col128, SIDE + QUART))
                win[at] = win[at] + tall
            return carry

        lax.fori_loop(0, SIDE // CHUNK, finish, 0, unroll=True)
        return carry

    lax.fori_loop(0, PAT, one_pattern, 0)

    for copy, base in outs:
        pl.when(touched(base))(copy.start)
    for copy, base in outs:
        copy.wait()


def run_patterns(where, strip, halo, probe, amps):
    form, flip = quarter_tables()
    hbm = pl.BlockSpec(memory_space=pl.ANY)
    vmem = pl.BlockSpec(memory_space=pltpu.VMEM)
    smem = pl.BlockSpec(memory_space=pltpu.SMEM)
    leads = [(2, 2)] * 6 + [(4, 3)] * 2
    part = [jax.ShapeDtypeStruct(lead + (SLICE, COLS), F32) for lead in leads]
    return pl.pallas_call(
        patterns_kernel,
        out_shape=part + [jax.ShapeDtypeStruct((2, SIDE, SIDE), F32)],
        in_specs=[smem] + [hbm] * 21,
        out_specs=[hbm] * 8 + [vmem],
        scratch_shapes=[
            pltpu.VMEM((2, SPAN, COLS), F32),
            pltpu.VMEM((2, SPAN, COLS), F32),
            pltpu.VMEM((2, SIDE, SIDE), F32),
            pltpu.VMEM((4, SIDE, 256), BF),
            pltpu.VMEM((4, SIDE, 256), BF),
            pltpu.VMEM((4, SIDE, 256), BF),
            pltpu.VMEM((4, SIDE, 256), BF),
            pltpu.VMEM((4 * SIDE, 256), F32),
            pltpu.VMEM((4 * SIDE, 256), F32),
            pltpu.VMEM((2, SIDE, SIDE), F32),
            pltpu.VMEM((PAT, SIDE, SIDE), F32),
            pltpu.VMEM((2, 4, 256, 256), BF),
            pltpu.VMEM((2, 4, 256, 256), BF),
            pltpu.SemaphoreType.DMA((80,)),
        ],
        compiler_params=pltpu.CompilerParams(vmem_limit_bytes=56 * 1024 * 1024),
        cost_estimate=pl.CostEstimate(flops=2 * 4_831_838_208, bytes_accessed=40_000_000, transcendentals=786_432),
    )(where, strip, *halo, probe, amps, jnp.asarray(form), jnp.asarray(flip))


def ring(axis, step):
    size = lax.axis_size(axis)
    return [(i, (i + step) % size) for i in range(size)]


def z_up(block):
    return lax.ppermute(block, "z", ring("z", 1))


def z_down(block):
    return lax.ppermute(block, "z", ring("z", -1))


def swap(block):
    return lax.ppermute(block, "core", [(0, 1), (1, 0)])


def along_tiles(block, step):
    tiles = lax.axis_size("x") * lax.axis_size("y")
    return lax.ppermute(block, ("x", "y"), [(i, i + step) for i in range(tiles) if 0 <= i + step < tiles])


def first_half(theirs, mine):
    both = mine + swap(theirs)
    return z_up(both[0]), z_down(both[1])


def second_half(both, from_below, from_above):
    last_below = z_up(both[0] + from_below[0])
    last_above = z_down(both[1] + from_above[1])
    return both[2] + from_above[0] + last_below, both[3] + from_below[1] + last_above


def others(block, axis):
    return [lax.ppermute(block, axis, ring(axis, -step)) for step in (1, 2, 3)]


def in_order(block, axis, rest=None):
    here = lax.axis_index(axis)
    four = jnp.stack([block] + (rest or others(block, axis)), axis=1)
    four = lax.dynamic_slice_in_dim(jnp.concatenate([four, four], axis=1), lax.rem(4 - here, 4), 4, 1)
    return four.reshape(2, -1, block.shape[2])


def share_of_sum(part, axis):
    here = lax.axis_index(axis)
    cut = part.reshape(2, 4, -1, part.shape[2])
    mine = lax.dynamic_index_in_dim(cut, here, 1, keepdims=False)
    return mine, [
        lax.ppermute(
            lax.dynamic_index_in_dim(cut, lax.rem(here + step, 4), 1, keepdims=False), axis, ring(axis, step)
        )
        for step in (1, 2, 3)
    ]


def on_device(object_field, probe, amplitudes, corners):
    z = lax.axis_index("z")
    core = lax.axis_index("core")
    tile = lax.axis_index("x") * lax.axis_size("y") + lax.axis_index("y")
    local = corners - jnp.array([1, 0], jnp.int32) * (tile * STRIP)
    where = jnp.concatenate([local.reshape(-1), jnp.stack([z, core]).astype(jnp.int32)])

    share = lax.dynamic_slice(
        object_field, (0, z * (2 * SLICE) + core * SLICE, 0), (2, SLICE, COLS)
    )
    order = jnp.asarray(order_matrix())
    product = functools.partial(jnp.einsum, precision=lax.Precision.HIGH)
    amps = product("nkl,ml->nkm", product("mk,nkl->nml", order, amplitudes), order)
    tie = lax.optimization_barrier
    re = along_tiles(share[0], -1)
    im = along_tiles(share[1], -1)
    below_re, above_re = z_up(re), z_down(re)
    below_im, above_im = z_up(im), z_down(im)
    below_re, above_re, amps = tie((below_re, above_re, amps))
    halo = [re, im, below_re, below_im, above_re, above_im, z_up(below_re), z_down(above_im)]
    halo += [swap(piece) for piece in halo]

    *sends, theirs2, mine2, probe_sum = run_patterns(where, object_field, halo, probe, amps)

    halves = probe_sum.reshape(2, 2, SIDE // 2, SIDE)
    part = lax.dynamic_index_in_dim(halves, core, 1, keepdims=False)
    part = part + swap(lax.dynamic_index_in_dim(halves, 1 - core, 1, keepdims=False))

    first_low = first_half(sends[4], sends[5])
    first_top = first_half(sends[0], sends[1])
    first_mid = first_half(sends[2], sends[3])
    both2 = mine2 + swap(theirs2)
    first_low, part = tie((first_low, part))
    low = second_half(both2[:, 2], *first_low)
    part, pieces = share_of_sum(part, "y")
    first_top, part, pieces = tie((first_top, part, pieces))
    part, pieces = share_of_sum(sum(pieces, part), "x")
    first_mid, part, pieces, low = tie((first_mid, part, pieces, low))
    carried = along_tiles(jnp.stack(low), 1)
    below, above = (jnp.stack(pair, axis=1) for pair in zip(first_top, first_mid))
    part = sum(pieces, part)
    below, above, part, pieces = tie((below, above, part, others(part, "z")))
    part = in_order(sum(pieces, part), "x")
    re, im = second_half(both2[:, :2], below, above)
    re, im, part, carried = tie((re, im, part, carried))

    re = re.at[0].add(carried[0])
    im = im.at[0].add(carried[1])
    re, im = tie((re, im))
    below_re, above_im = z_up(re), z_down(im)
    below_im, above_re = z_up(im), z_down(re)
    opposite_re, opposite_im = z_up(below_re), z_down(above_im)
    found = (
        (re, 0, 0), (im, 1, 0),
        (below_re, 0, 3), (above_im, 1, 1), (below_im, 1, 3), (above_re, 0, 1),
        (opposite_re, 0, 2), (opposite_im, 1, 2),
    )
    opposite_re, opposite_im, part, pieces = tie((opposite_re, opposite_im, part, others(part, "y")))
    part = in_order(part, "y", pieces)
    other = swap(part)
    probe_gradient = jnp.concatenate([
        jnp.where(core == 0, part, other), jnp.where(core == 0, other, part)
    ], axis=1)
    whole = jnp.zeros((2, 2, 4, 2, SLICE, COLS), F32)

    def put(whole, block, plane, shift, owner):
        at = (plane, 0, lax.rem(z + shift, 4), owner, 0, 0)
        return lax.dynamic_update_slice(whole, block[None, :, None, None], at)

    for group in (found[:6], found[6:]):
        for block, plane, shift in group:
            whole = put(whole, block, plane, shift, core)
        for block, plane, shift in group:
            whole = put(whole, swap(block), plane, shift, 1 - core)
    return (whole.reshape(2, STRIP, COLS), probe_gradient)


def solution(mesh):
    tiles, scans = mesh.devices.shape
    side = math.isqrt(tiles)
    fine = Mesh(mesh.devices.reshape(side, tiles // side, scans // 2, 2), ("x", "y", "z", "core"))
    placed = (
        P(None, ("x", "y"), None),
        P(),
        P(("x", "y", "z", "core"), None, None),
        P(("x", "y", "z", "core"), None),
    )
    return jax.shard_map(
        on_device,
        mesh=fine,
        in_specs=placed,
        out_specs=(P(None, ("x", "y"), None), P()),
        check_vma=False,
    )
```
